128 devices in a mesh: lev: 4 (over y), col: 32 (over x, z, core).
Axes of the slice: x: 4, y: 4, z: 4, core: 2. Of those that a mesh axis runs over, the one named last changes fastest.
Arguments:
- increment: bfloat16 [3, 128, 131072], P(None, 'lev', 'col'), may hold values from -6 to 6
- jacobian: bfloat16 [1024, 616, 384], P(('lev', 'col')), may hold values from -0.3125 to 0.3125
- departure: bfloat16 [616, 1048576], P(None, ('lev', 'col')), may hold values from -6 to 6
- predictor: float32 [8, 1048576], P(None, ('lev', 'col')), may hold values from -5 to 5
- bias_coef: float32 [616, 8], replicated, may hold values from -1.5 to 1.5
- obs_sigma: float32 [616], replicated, may hold values from 0.5 to 2
- channel_use: int32 [1024, 616], P(('lev', 'col')), may hold values 0 or 1
- send_cols: int32 [128, 128, 8], P(('lev', 'col')), may hold values from 0 to 1023
- obs_slot: int32 [1048576], P(('lev', 'col')), may hold values from 0 to 1023, as said below
Outputs:
- gradient: float32 [3, 128, 131072], P(None, 'lev', 'col')
The draws below stay inside these ranges and needn't reach their ends.
Inputs may be any that keep to these rules, and one draw needn't show every extreme that they name: obs_slot[j] = s * 8 + k; the slots (s, p, k) named by the observations of device p are, for each s, the first few of the 8, at least 2 of them; some device p names all 8 slots of every device.
All inputs are finite; a program needn't handle non-finite values. No bound on the sum of `channel_use` on one device may be relied on, other than what follows from the above.
Results may differ from the reference program's by a relative error of at most 0.001.
Values may be sent and summed in bfloat16 or wider, within the bound.
A program may use at most 128 MiB of HBM per device.

```python
import math
import jax
import jax.numpy as jnp
from jax import lax

NF = 3
LEV = 128
CHAN = 616
NPRED = 8
COLS_DEV = 1024
CAP = 8
OBS_TILE = 1024
TILES_DEV = 8
GROUPS = 4
SHARDS = 32
NDEV = 128
OBS_DEV = 8192
NCOL = 131072
NTILES = 1024
NOBS = 1048576


def slot_plan(key):
    base_key = jax.random.fold_in(key, 7)
    count_key, full_key = jax.random.split(base_key)
    counts = jax.random.randint(count_key, (NDEV, NDEV), CAP // 4, CAP + 1, dtype=jnp.int32)
    receiver = jax.random.randint(full_key, (), 0, NDEV, dtype=jnp.int32)
    filled = jnp.arange(NDEV, dtype=jnp.int32)[None, :] == receiver
    return (jnp.where(filled, jnp.int32(CAP), counts), receiver)


def draw_send_cols(key, part):
    list_key = jax.random.fold_in(key, 11)
    return jax.random.randint(list_key, (NDEV, NDEV, CAP), 0, COLS_DEV, dtype=jnp.int32)


def draw_obs_slot(key, part):
    counts, receiver = slot_plan(key)
    source_key, offset_key = jax.random.split(jax.random.fold_in(key, 13))
    positions = jnp.arange(NOBS, dtype=jnp.int32)
    holder = positions // OBS_DEV
    source = jax.random.randint(source_key, (NOBS,), 0, NDEV, dtype=jnp.int32)
    raw_offset = jax.random.randint(offset_key, (NOBS,), 0, 1 << 20, dtype=jnp.int32)
    offset = raw_offset % counts[source, holder]
    slots = (source * CAP + offset).astype(jnp.int32)
    first = receiver * OBS_DEV
    slots = jnp.where(positions == first, jnp.int32(NDEV * CAP - 1), slots)
    slots = jnp.where(positions == first + 1, jnp.int32(0), slots)
    return slots.astype(jnp.int32)


def plant(array, own_key, smallest, high):
    spot = [jax.random.randint(jax.random.fold_in(own_key, axis), (), 0, length) for axis, length in enumerate(array.shape)]
    main_axis = array.shape.index(max(array.shape))
    neighbour = spot[:main_axis] + [(spot[main_axis] + 1) % array.shape[main_axis]] + spot[main_axis + 1:]
    return array.at[tuple(spot)].set(smallest).at[tuple(neighbour)].set(high)


def levels(stream_key, extent, cuts, least, largest):
    def one(axis_at, shards_of):
        heights = jax.random.uniform(jax.random.fold_in(jax.random.fold_in(stream_key, 6), axis_at), (shards_of,), jnp.float32, least / len(cuts), largest / len(cuts))
        return jnp.repeat(jnp.exp(heights), extent[axis_at] // shards_of).reshape((-1,) + (1,) * (len(extent) - axis_at - 1))

    factor_of = one(*cuts[0])
    for cut in cuts[1:]:
        factor_of = factor_of * one(*cut)
    return factor_of


def noise(stream_key, dims, width, limit, cuts=(), kind=jnp.bfloat16):
    gain = levels(stream_key, dims, cuts, -0.22, 0.18) if cuts else 1.0
    entries = jax.random.normal(stream_key, dims, jnp.float32) * width * gain
    return jnp.minimum(jnp.maximum(entries, -limit), limit).astype(kind)


def setup_inputs(seed: int = 0) -> dict:
    streams_of = jax.random.split(jax.random.key(seed), 10)
    increment = noise(streams_of[0], (NF, LEV, NCOL), 1.0, 6.0, ((1, 4), (2, 32)))
    jacobian = noise(streams_of[1], (NTILES, CHAN, NF * LEV), (NF * LEV) ** -0.5, 0.3125, ((0, 128),))
    departure = noise(streams_of[2], (CHAN, NOBS), 1.0, 6.0, ((1, 128),))
    predictor = noise(streams_of[3], (NPRED, NOBS), 1.0, 5.0, ((1, 128),), jnp.float32)
    bias_coef = noise(streams_of[4], (CHAN, NPRED), 0.3, 1.5, (), jnp.float32)
    obs_sigma = jnp.clip(jnp.exp(jax.random.uniform(streams_of[5], (CHAN,), jnp.float32, math.log(0.5), math.log(2.0))), 0.5, 2.0)
    channel_use = plant((jax.random.randint(streams_of[6], (NTILES, CHAN), 0, 4) < 3).astype(jnp.int32), jax.random.fold_in(streams_of[6], 1), 0, 1)
    send_cols = draw_send_cols(jax.random.fold_in(streams_of[9], 71), 0)
    obs_slot = draw_obs_slot(jax.random.fold_in(streams_of[9], 71), 0)
    return {"increment": increment, "jacobian": jacobian, "departure": departure, "predictor": predictor, "bias_coef": bias_coef, "obs_sigma": obs_sigma, "channel_use": channel_use, "send_cols": send_cols, "obs_slot": obs_slot}


def reference(increment, jacobian, departure, predictor, bias_coef, obs_sigma, channel_use, send_cols, obs_slot):
    profile_len = NF * LEV
    columns_major = increment.reshape(profile_len, NCOL).T
    owners = jnp.arange(NDEV, dtype=jnp.int32)
    owner_base = ((owners % SHARDS) * GROUPS * COLS_DEV + (owners // SHARDS) * COLS_DEV).astype(jnp.int32)
    column_map = owner_base[:, None, None] + send_cols.astype(jnp.int32)
    inverse_var = 1.0 / (obs_sigma * obs_sigma)

    def visit(total, device):
        start = (device * OBS_DEV).astype(jnp.int32)
        slots = lax.dynamic_slice_in_dim(obs_slot, start, OBS_DEV)
        source = slots // CAP
        offset = slots % CAP
        target = column_map[source, device, offset].astype(jnp.int32)
        profile = columns_major[target]
        blocks = lax.dynamic_slice_in_dim(jacobian, (device * TILES_DEV).astype(jnp.int32), TILES_DEV, 0).astype(jnp.float32)
        tangent = jnp.einsum('tcf,tof->cto', blocks, profile.reshape(TILES_DEV, OBS_TILE, profile_len).astype(jnp.float32))
        observed = lax.dynamic_slice_in_dim(departure, start, OBS_DEV, 1).astype(jnp.float32)
        preds = lax.dynamic_slice_in_dim(predictor, start, OBS_DEV, 1)
        bias_term = jnp.dot(bias_coef, preds, precision=lax.Precision.HIGHEST, preferred_element_type=jnp.float32)
        residual = tangent - (observed - bias_term).reshape(CHAN, TILES_DEV, OBS_TILE)
        usage = lax.dynamic_slice_in_dim(channel_use, (device * TILES_DEV).astype(jnp.int32), TILES_DEV, 0).astype(jnp.float32).T
        scaling = usage * inverse_var[:, None]
        forcing = (scaling[:, :, None] * residual).astype(jnp.bfloat16)
        adjoint = jnp.einsum('tcf,cto->tof', blocks, forcing.astype(jnp.float32)).reshape(OBS_DEV, profile_len)
        total = total.at[target].add(adjoint)
        return total, None

    start_total = jnp.zeros((NCOL, profile_len), jnp.float32)
    total, unused = lax.scan(visit, start_total, jnp.arange(NDEV, dtype=jnp.int32))
    return total.T.reshape(NF, LEV, NCOL)
```

```python
import functools

import jax
import jax.numpy as jnp
from jax import lax
from jax.experimental import pallas as pl
from jax.experimental.pallas import tpu as pltpu
from jax.sharding import PartitionSpec as P

MESH = pl.DeviceIdType.MESH
NF = 3
LEVD = 4
COLD = 32
NDEV = LEVD * COLD
SLAB = 32
ROWS = NF * SLAB
PROF = ROWS * LEVD
CAP = 8
SLOTS = NDEV * CAP
COLS = 1024
CHAN = 616
CPAD = 640
NPRED = 8
TILE = 1024
TILES = 8
OBS = TILE * TILES
F32 = jnp.float32
BF16 = jnp.bfloat16


def peer_id(index):
    return (index // COLD, lax.rem(index, COLD))


def one_hot(row, block):
    local = jnp.broadcast_to((row - 256.0 * block), (256, 128)).astype(BF16)
    index = lax.broadcasted_iota(jnp.int32, (256, 128), 0).astype(F32).astype(BF16)
    return jnp.where(index == local, jnp.ones((), BF16), jnp.zeros((), BF16))


def split3(value):
    high = value.astype(BF16).astype(F32)
    rest = value - high
    mid = rest.astype(BF16).astype(F32)
    return high, mid, (rest - mid).astype(BF16).astype(F32)


def kernel(
    inc_hbm, jac_hbm, dep_hbm, pred_hbm, coef_hbm, sigma_hbm, use_hbm, cols_hbm, slot_hbm,
    out_ref,
    inc, dep, pred, coef, sigma, use, cols, slot,
    lists, hot, gath, sendb, recvb, xt, xaug, jaug, jt, paug, scale, square, forcing,
    adj, acc, rsend, rrecv, yt,
    in_sem, dep_sem, list_send, list_recv, send_sem, recv_sem, rsend_sem, rrecv_sem, own_sem,
):
    lev = lax.axis_index("lev")
    col = lax.axis_index("col")
    me = lev * COLD + col
    barrier = pltpu.get_barrier_semaphore()

    loads = [
        pltpu.make_async_copy(src, dst, in_sem.at[i])
        for i, (src, dst) in enumerate(
            (
                (cols_hbm, cols), (inc_hbm, inc), (slot_hbm, slot), (jac_hbm, jaug.at[:, :, pl.ds(0, PROF)]), (pred_hbm, pred),
                (coef_hbm, coef), (sigma_hbm, sigma), (use_hbm, use),
            )
        )
    ]
    for load in loads:
        load.start()

    def dep_load(t):
        at = pl.multiple_of(t * TILE, TILE)
        return pltpu.make_async_copy(
            dep_hbm.at[:, pl.ds(at, TILE)], dep.at[lax.rem(t, 2)], dep_sem.at[lax.rem(t, 2)]
        )

    dep_load(0).start()

    def greet(i, carry):
        pl.semaphore_signal(barrier, inc=1, device_id=peer_id(lax.rem(me + i, NDEV)), device_id_type=MESH)
        return carry

    lax.fori_loop(1, NDEV, greet, 0)

    loads[0].wait()
    square[...] = jnp.zeros_like(square)
    square[0:NDEV, 0:CAP] = cols[...].astype(F32)
    lists[lev] = square[0:128, :].T[0:CAP, :].astype(jnp.int32)
    pl.semaphore_wait(barrier, NDEV - 1)

    def list_copy(i):
        other = lax.rem(lev + i, LEVD)
        return pltpu.make_async_remote_copy(
            src_ref=lists.at[lev], dst_ref=lists.at[lev], send_sem=list_send.at[i],
            recv_sem=list_recv.at[i], device_id=(other, col), device_id_type=MESH,
        )

    for i in range(1, LEVD):
        list_copy(i).start()
    loads[1].wait()

    def build_pick(owner):
        def build(k, carry):
            row = lists[owner, pl.ds(k, 1), :].astype(F32)
            at = pl.multiple_of(owner * SLOTS + k * 128, 128)
            for b in range(4):
                hot[b * 256 : (b + 1) * 256, pl.ds(at, 128)] = one_hot(row, b)
            return carry

        lax.fori_loop(0, CAP, build, 0)

    for i in range(LEVD):
        owner = lax.rem(lev + (LEVD - i), LEVD)
        if i:
            list_copy(i).wait_recv()

        build_pick(owner)
        at = pl.multiple_of(owner * COLS, COLS)
        to = pl.multiple_of(owner * ROWS, 32)
        gath[pl.ds(to, ROWS), :] = jnp.dot(
            inc[:, pl.ds(at, COLS)], hot[:, pl.ds(at, SLOTS)], preferred_element_type=F32
        )
    for i in range(1, LEVD):
        list_copy(i).wait_send()
    for k in range(CAP):
        for m in range(NF):
            rsend[m, pl.ds(k, NDEV, stride=CAP), :] = gath[m * 128 : (m + 1) * 128, k * 128 : (k + 1) * 128].T
    for m in range(NF):
        sendb[:, :, m * 128 : (m + 1) * 128] = rsend[m].reshape(NDEV, CAP, 128).astype(BF16)

    own = pltpu.make_async_copy(sendb.at[me], recvb.at[me], own_sem.at[0])
    own.start()

    def fetch(i, carry):
        other = lax.rem(me + i, NDEV)
        pltpu.make_async_remote_copy(
            src_ref=sendb.at[other], dst_ref=recvb.at[me], send_sem=send_sem, recv_sem=recv_sem,
            device_id=peer_id(other), device_id_type=MESH,
        ).start()
        return carry

    lax.fori_loop(1, NDEV, fetch, 0)

    for load in loads[2:]:
        load.wait()

    def build_hot(m, carry):
        row = slot[pl.ds(m, 1), :].astype(F32)
        at = pl.multiple_of(m * 128, 128)
        for b in range(4):
            hot[b * 256 : (b + 1) * 256, pl.ds(at, 128)] = one_hot(row, b)
        return carry

    lax.fori_loop(0, OBS // 128, build_hot, 0)

    inverse = 1.0 / (sigma[...] * sigma[...])
    square[...] = jnp.zeros_like(square)
    wide = jnp.concatenate(
        [use[...].astype(F32) * inverse, jnp.zeros((TILES, CPAD - CHAN), F32)], axis=1
    )
    for m in range(CPAD // 128):
        square[0:TILES, :] = wide[:, m * 128 : (m + 1) * 128]
        turned = square[0:128, :].T
        for t in range(TILES):
            scale[t, m * 128 : (m + 1) * 128, :] = jnp.broadcast_to(turned[:, t : t + 1], (128, 128))

    high, mid, low = split3(pred[...])
    paug[...] = jnp.zeros_like(paug)
    paug[0:48, :] = jnp.concatenate([high, mid, low, high, mid, high], axis=0).astype(BF16)
    repeat = (
        lax.broadcasted_iota(jnp.int32, (NPRED, 128), 0)
        == lax.rem(lax.broadcasted_iota(jnp.int32, (NPRED, 128), 1), NPRED)
    ).astype(F32)
    tiled = jnp.dot(coef[...], repeat, precision=lax.Precision.HIGHEST, preferred_element_type=F32)
    ch, cm, cl = split3(tiled)
    lane = lax.broadcasted_iota(jnp.int32, (CHAN, 128), 1)
    ccoef = jnp.where(lane < 24, ch, jnp.where(lane < 40, cm, jnp.where(lane < 48, cl, 0.0)))

    forcing[...] = jnp.zeros_like(forcing)
    for t in range(TILES):
        jaug[t, :, PROF : PROF + 128] = ccoef.astype(BF16)

    def turn(t, carry):
        tall = jnp.concatenate([jaug[t, :, 0:PROF].astype(F32), jnp.zeros((CPAD - CHAN, PROF), F32)], axis=0)
        jt[t] = tall.T.astype(BF16)
        return carry

    lax.fori_loop(0, TILES, turn, 0)

    pltpu.make_async_copy(sendb.at[pl.ds(0, NDEV - 1)], sendb.at[pl.ds(0, NDEV - 1)], send_sem).wait()
    pltpu.make_async_copy(recvb.at[pl.ds(0, NDEV - 1)], recvb.at[pl.ds(0, NDEV - 1)], recv_sem).wait()
    own.wait()
    for h in range(LEVD):
        got = recvb[h * COLD : (h + 1) * COLD].astype(F32).reshape(COLD * CAP, PROF)
        turned = got.T.astype(BF16)
        for owner in range(LEVD):
            for field in range(NF):
                xt[field * 128 + h * SLAB : field * 128 + (h + 1) * SLAB, owner * 256 : (owner + 1) * 256] = turned[
                    owner * ROWS + field * SLAB : owner * ROWS + (field + 1) * SLAB, :
                ]

    def observe(t, carry):
        @pl.when(t + 1 < TILES)
        def _():
            dep_load(t + 1).start()

        at = pl.multiple_of(t * TILE, TILE)
        xaug[0:PROF, :] = jnp.dot(xt[...], hot[:, pl.ds(at, TILE)], preferred_element_type=F32).astype(BF16)
        xaug[PROF : PROF + 128, :] = paug[:, pl.ds(at, TILE)]
        dep_load(t).wait()
        half = lax.rem(t, 2)
        for n in range(TILE // 256):
            lanes = slice(n * 256, (n + 1) * 256)
            tangent = jnp.dot(jaug[t], xaug[:, lanes], preferred_element_type=F32)
            factor = scale[t, 0:CHAN, :]
            residual = tangent - dep[half, :, lanes].astype(F32)
            forcing[0:CHAN, lanes] = (jnp.concatenate([factor, factor], axis=1) * residual).astype(BF16)
        for n in range(TILE // 256):
            lanes = slice(n * 256, (n + 1) * 256)
            to = pl.multiple_of(at + n * 256, 256)
            value = jnp.dot(jt[t], forcing[:, lanes], preferred_element_type=F32)
            first = value.astype(BF16)
            second = (value - first.astype(F32)).astype(BF16)
            for h in range(LEVD):
                for field in range(NF):
                    rows = slice(field * 128 + h * SLAB, field * 128 + (h + 1) * SLAB)
                    put = slice(field * SLAB, (field + 1) * SLAB)
                    adj[h, 0, put, pl.ds(to, 256)] = first[rows, :]
                    adj[h, 1, put, pl.ds(to, 256)] = second[rows, :]
        return carry

    lax.fori_loop(0, TILES, observe, 0)

    def give_back(step, carry):
        pair = lax.rem(lev // 2 + step // 2, 2)
        half = lax.rem(col // 16 + step, 2)
        acc[...] = jnp.zeros_like(acc)

        def add(t, inner):
            at = pl.multiple_of(t * TILE, TILE)
            left = adj[pl.ds(pair * 2, 2), :, :, pl.ds(at, TILE)].reshape(4 * ROWS, TILE)
            for owner in range(LEVD):
                rows = pl.multiple_of(owner * 256 + half * 128, 128)
                acc[:, owner * 128 : (owner + 1) * 128] += lax.dot_general(
                    left, hot[pl.ds(rows, 128), pl.ds(at, TILE)], (((1,), (1,)), ((), ())),
                    preferred_element_type=F32,
                )
            return inner

        lax.fori_loop(0, TILES, add, 0)
        for h in range(2):
            total = acc[h * 192 : h * 192 + ROWS, :] + acc[h * 192 + ROWS : (h + 1) * 192, :]
            tall = jnp.concatenate([total[:, o * 128 : (o + 1) * 128] for o in range(LEVD)], axis=0)
            to = pl.multiple_of(((pair * 2 + h) * COLD + half * 16) * CAP, 128)
            for m in range(NF):
                rsend[m, pl.ds(to, 128), :] = tall[m * 128 : (m + 1) * 128, :].T

        def push(i, inner):
            other = (pair * 2 + i // 16) * COLD + half * 16 + lax.rem(i + col, 16)
            src = rsend.at[:, pl.ds(pl.multiple_of(other * CAP, CAP), CAP), :]
            dst = rrecv.at[:, pl.ds(pl.multiple_of(me * CAP, CAP), CAP), :]

            @pl.when(other != me)
            def _():
                pltpu.make_async_remote_copy(
                    src_ref=src, dst_ref=dst, send_sem=rsend_sem, recv_sem=rrecv_sem,
                    device_id=peer_id(other), device_id_type=MESH,
                ).start()

            @pl.when(other == me)
            def _():
                pltpu.make_async_copy(src, dst, own_sem.at[1]).start()

            return inner

        lax.fori_loop(0, 32, push, 0)
        return carry

    lax.fori_loop(0, 4, give_back, 0)
    for owner in range(LEVD):
        build_pick(owner)
    mine = pl.ds(pl.multiple_of(me * CAP, CAP), CAP)
    pltpu.make_async_copy(rsend.at[:, mine, :], rrecv.at[:, mine, :], own_sem.at[1]).wait()
    most = pl.ds(0, SLOTS - CAP)
    pltpu.make_async_copy(rsend.at[:, most, :], rsend.at[:, most, :], rsend_sem).wait()
    pltpu.make_async_copy(rrecv.at[:, most, :], rrecv.at[:, most, :], rrecv_sem).wait()

    for k in range(CAP):
        value = jnp.concatenate([rrecv[m, pl.ds(k, NDEV, stride=CAP), :].T for m in range(NF)], axis=0)
        first = value.astype(BF16)
        second = (value - first.astype(F32)).astype(BF16)
        lanes = slice(k * 128, (k + 1) * 128)
        for owner in range(LEVD):
            rows = slice(owner * ROWS, (owner + 1) * ROWS)
            yt[owner, 0:ROWS, lanes] = first[rows, :]
            yt[owner, ROWS : 2 * ROWS, lanes] = second[rows, :]
    for owner in range(LEVD):
        both = lax.dot_general(
            yt[owner], hot[:, owner * SLOTS : (owner + 1) * SLOTS], (((1,), (1,)), ((), ())), preferred_element_type=F32
        )
        out_ref[:, owner * COLS : (owner + 1) * COLS] = both[0:ROWS, :] + both[ROWS : 2 * ROWS, :]


def on_device(increment, jacobian, departure, predictor, bias_coef, obs_sigma, channel_use, send_cols, obs_slot):
    out = pl.pallas_call(
        kernel,
        out_shape=jax.ShapeDtypeStruct((ROWS, LEVD * COLS), F32),
        in_specs=[pl.BlockSpec(memory_space=pl.ANY)] * 9,
        out_specs=pl.BlockSpec(memory_space=pltpu.VMEM),
        scratch_shapes=[
            pltpu.VMEM((ROWS, LEVD * COLS), BF16),
            pltpu.VMEM((2, CHAN, TILE), BF16),
            pltpu.VMEM((NPRED, OBS), F32),
            pltpu.VMEM((CHAN, NPRED), F32),
            pltpu.VMEM((1, CHAN), F32),
            pltpu.VMEM((TILES, CHAN), jnp.int32),
            pltpu.VMEM((NDEV, CAP), jnp.int32),
            pltpu.VMEM((OBS // 128, 128), jnp.int32),
            pltpu.VMEM((LEVD, CAP, NDEV), jnp.int32),
            pltpu.VMEM((SLOTS, OBS), BF16),
            pltpu.VMEM((PROF, SLOTS), F32),
            pltpu.VMEM((NDEV, CAP, PROF), BF16),
            pltpu.VMEM((NDEV, CAP, PROF), BF16),
            pltpu.VMEM((PROF, SLOTS), BF16),
            pltpu.VMEM((PROF + 128, TILE), BF16),
            pltpu.VMEM((TILES, CHAN, PROF + 128), BF16),
            pltpu.VMEM((TILES, PROF, CPAD), BF16),
            pltpu.VMEM((128, OBS), BF16),
            pltpu.VMEM((TILES, CPAD, 128), F32),
            pltpu.VMEM((128, 128), F32),
            pltpu.VMEM((CPAD, TILE), BF16),
            pltpu.VMEM((LEVD, 2, ROWS, OBS), BF16),
            pltpu.VMEM((4 * ROWS, 512), F32),
            pltpu.VMEM((NF, SLOTS, 128), F32),
            pltpu.VMEM((NF, SLOTS, 128), F32),
            pltpu.VMEM((LEVD, 2 * ROWS, SLOTS), BF16),
            pltpu.SemaphoreType.DMA((8,)),
            pltpu.SemaphoreType.DMA((2,)),
            pltpu.SemaphoreType.DMA((LEVD,)),
            pltpu.SemaphoreType.DMA((LEVD,)),
            pltpu.SemaphoreType.DMA,
            pltpu.SemaphoreType.DMA,
            pltpu.SemaphoreType.DMA,
            pltpu.SemaphoreType.DMA,
            pltpu.SemaphoreType.DMA((2,)),
        ],
        compiler_params=pltpu.CompilerParams(
            collective_id=0, has_side_effects=True, vmem_limit_bytes=63 * 2**20
        ),
    )(
        increment.reshape(ROWS, LEVD * COLS),
        jacobian,
        departure,
        predictor,
        bias_coef,
        obs_sigma.reshape(1, CHAN),
        channel_use,
        send_cols.reshape(NDEV, CAP),
        obs_slot.reshape(OBS // 128, 128),
    )
    return out.reshape(NF, SLAB, LEVD * COLS)


def solution(mesh):
    return jax.shard_map(
        on_device,
        mesh=mesh,
        in_specs=(
            P(None, "lev", "col"),
            P(("lev", "col"), None, None),
            P(None, ("lev", "col")),
            P(None, ("lev", "col")),
            P(),
            P(),
            P(("lev", "col"), None),
            P(("lev", "col"), None, None),
            P(("lev", "col")),
        ),
        out_specs=P(None, "lev", "col"),
        check_vma=False,
    )
```

```python
import functools

import jax
import jax.numpy as jnp
from jax import lax
from jax.experimental import pallas as pl
from jax.experimental.pallas import tpu as pltpu
from jax.sharding import PartitionSpec as P

MESH = pl.DeviceIdType.MESH
NF = 3
LEVD = 4
COLD = 32
NDEV = LEVD * COLD
SLAB = 32
ROWS = NF * SLAB
PROF = ROWS * LEVD
CAP = 8
SLOTS = NDEV * CAP
COLS = 1024
CHAN = 616
CPAD = 640
NPRED = 8
TILE = 1024
TILES = 8
OBS = TILE * TILES
F32 = jnp.float32
BF16 = jnp.bfloat16


def peer_id(index):
    return (index // COLD, lax.rem(index, COLD))


def one_hot(row, block):
    local = jnp.broadcast_to((row - 256.0 * block), (256, 128)).astype(BF16)
    index = lax.broadcasted_iota(jnp.int32, (256, 128), 0).astype(F32).astype(BF16)
    return jnp.where(index == local, jnp.ones((), BF16), jnp.zeros((), BF16))


def split3(value):
    high = value.astype(BF16).astype(F32)
    rest = value - high
    mid = rest.astype(BF16).astype(F32)
    return high, mid, (rest - mid).astype(BF16).astype(F32)


def kernel(
    inc_hbm, jac_hbm, dep_hbm, pred_hbm, coef_hbm, sigma_hbm, use_hbm, cols_hbm, slot_hbm,
    out_ref,
    inc, dep, pred, coef, sigma, use, slot,
    lists, hot, gath, sendb, recvb, xt, xaug, jaug, jt, paug, scale, square, forcing,
    adj, acc, rsend, rrecv, units_out, units_in, rows8, yt,
    in_sem, dep_sem, list_send, list_recv, send_sem, recv_sem, rsend_sem, rrecv_sem, msend_sem, mrecv_sem, all_sem, own_sem,
):
    lev = lax.axis_index("lev")
    col = lax.axis_index("col")
    me = lev * COLD + col
    barrier = pltpu.get_barrier_semaphore()

    loads = [
        pltpu.make_async_copy(src, dst, in_sem.at[i])
        for i, (src, dst) in enumerate(
            (
                (cols_hbm, lists.at[lev]), (inc_hbm, inc), (slot_hbm, slot), (jac_hbm, jaug.at[:, :, pl.ds(0, PROF)]), (pred_hbm, pred),
                (coef_hbm, coef), (sigma_hbm, sigma), (use_hbm, use),
            )
        )
    ]
    for load in loads:
        load.start()

    def dep_load(t):
        at = pl.multiple_of(t * TILE, TILE)
        return pltpu.make_async_copy(
            dep_hbm.at[:, pl.ds(at, TILE)], dep.at[lax.rem(t, 2)], dep_sem.at[lax.rem(t, 2)]
        )

    dep_load(0).start()

    place = col // 2
    core = lax.rem(col, 2)

    def near(i):
        return (lax.rem(lev + i // 2, LEVD), place * 2 + lax.rem(core + i, 2))

    def far(i):
        return (lev, lax.rem(place + i, COLD // 2) * 2 + core)

    for i in range(1, 2 * LEVD):
        pl.semaphore_signal(barrier, inc=1, device_id=near(i), device_id_type=MESH)
    for i in range(1, COLD // 2):
        pl.semaphore_signal(barrier, inc=1, device_id=far(i), device_id_type=MESH)
    loads[0].wait()
    pl.semaphore_wait(barrier, 2 * LEVD - 1 + COLD // 2 - 1)

    def list_copy(i):
        other = lax.rem(lev + i, LEVD)
        return pltpu.make_async_remote_copy(
            src_ref=lists.at[lev], dst_ref=lists.at[lev], send_sem=list_send.at[i],
            recv_sem=list_recv.at[i], device_id=(other, col), device_id_type=MESH,
        )

    for i in range(1, LEVD):
        list_copy(i).start()
    for i in range(1, 2 * LEVD):
        pl.semaphore_signal(all_sem, inc=1, device_id=near(i), device_id_type=MESH)
    loads[1].wait()

    def build_pick(owner):
        def build(k, carry):
            row = lists[owner, pl.ds(k, 1), :].astype(F32)
            at = pl.multiple_of(owner * SLOTS + k * 128, 128)
            for b in range(4):
                hot[b * 256 : (b + 1) * 256, pl.ds(at, 128)] = one_hot(row, b)
            return carry

        lax.fori_loop(0, CAP, build, 0)

    for i in range(LEVD):
        owner = lax.rem(lev + (LEVD - i), LEVD)
        if i:
            list_copy(i).wait_recv()

        build_pick(owner)
        at = pl.multiple_of(owner * COLS, COLS)
        to = pl.multiple_of(owner * ROWS, 32)
        gath[pl.ds(to, ROWS), :] = jnp.dot(
            inc[:, pl.ds(at, COLS)], hot[:, pl.ds(at, SLOTS)], preferred_element_type=F32
        )
    for i in range(1, LEVD):
        list_copy(i).wait_send()
    for k in range(CAP):
        for m in range(NF):
            rows8[m, pl.ds(k, NDEV, stride=CAP), :] = gath[m * 128 : (m + 1) * 128, k * 128 : (k + 1) * 128].T
    for m in range(NF):
        sendb[:, :, m * 128 : (m + 1) * 128] = rows8[m].reshape(NDEV, CAP, 128).astype(BF16)

    pl.semaphore_wait(all_sem, 2 * LEVD - 1)
    own = pltpu.make_async_copy(sendb.at[me], recvb.at[me], own_sem.at[0])
    own.start()

    def fetch(i, carry):
        other = lax.rem(me + i, NDEV)
        pltpu.make_async_remote_copy(
            src_ref=sendb.at[other], dst_ref=recvb.at[me], send_sem=send_sem, recv_sem=recv_sem,
            device_id=peer_id(other), device_id_type=MESH,
        ).start()
        return carry

    lax.fori_loop(1, NDEV, fetch, 0)

    for load in loads[2:]:
        load.wait()

    def build_hot(m, carry):
        row = slot[pl.ds(m, 1), :].astype(F32)
        at = pl.multiple_of(m * 128, 128)
        for b in range(4):
            hot[b * 256 : (b + 1) * 256, pl.ds(at, 128)] = one_hot(row, b)
        return carry

    lax.fori_loop(0, OBS // 128, build_hot, 0)

    deviation = sigma[...].reshape(1, CHAN)
    inverse = 1.0 / (deviation * deviation)
    square[...] = jnp.zeros_like(square)
    wide = jnp.concatenate(
        [use[...].astype(F32) * inverse, jnp.zeros((TILES, CPAD - CHAN), F32)], axis=1
    )
    for m in range(CPAD // 128):
        square[0:TILES, :] = wide[:, m * 128 : (m + 1) * 128]
        turned = square[0:128, :].T
        for t in range(TILES):
            scale[t, m * 128 : (m + 1) * 128, :] = jnp.broadcast_to(turned[:, t : t + 1], (128, 128))

    high, mid, low = split3(pred[...])
    paug[...] = jnp.zeros_like(paug)
    paug[0:48, :] = jnp.concatenate([high, mid, low, high, mid, high], axis=0).astype(BF16)
    repeat = (
        lax.broadcasted_iota(jnp.int32, (NPRED, 128), 0)
        == lax.rem(lax.broadcasted_iota(jnp.int32, (NPRED, 128), 1), NPRED)
    ).astype(F32)
    tiled = lax.dot_general(
        coef[...], repeat, (((0,), (0,)), ((), ())), precision=lax.Precision.HIGHEST, preferred_element_type=F32
    )
    ch, cm, cl = split3(tiled)
    lane = lax.broadcasted_iota(jnp.int32, (CHAN, 128), 1)
    ccoef = jnp.where(lane < 24, ch, jnp.where(lane < 40, cm, jnp.where(lane < 48, cl, 0.0)))

    forcing[...] = jnp.zeros_like(forcing)
    for t in range(TILES):
        jaug[t, :, PROF : PROF + 128] = ccoef.astype(BF16)

    def turn(t, carry):
        tall = jnp.concatenate([jaug[t, :, 0:PROF].astype(F32), jnp.zeros((CPAD - CHAN, PROF), F32)], axis=0)
        jt[t] = tall.T.astype(BF16)
        return carry

    lax.fori_loop(0, TILES, turn, 0)

    pltpu.make_async_copy(sendb.at[pl.ds(0, NDEV - 1)], sendb.at[pl.ds(0, NDEV - 1)], send_sem).wait()
    pltpu.make_async_copy(recvb.at[pl.ds(0, NDEV - 1)], recvb.at[pl.ds(0, NDEV - 1)], recv_sem).wait()
    own.wait()
    for h in range(LEVD):
        got = recvb[h * COLD : (h + 1) * COLD].astype(F32).reshape(COLD * CAP, PROF)
        turned = got.T.astype(BF16)
        for owner in range(LEVD):
            for field in range(NF):
                xt[field * 128 + h * SLAB : field * 128 + (h + 1) * SLAB, owner * 256 : (owner + 1) * 256] = turned[
                    owner * ROWS + field * SLAB : owner * ROWS + (field + 1) * SLAB, :
                ]

    def observe(t, carry):
        @pl.when(t + 1 < TILES)
        def _():
            dep_load(t + 1).start()

        at = pl.multiple_of(t * TILE, TILE)
        xaug[0:PROF, :] = jnp.dot(xt[...], hot[:, pl.ds(at, TILE)], preferred_element_type=F32).astype(BF16)
        xaug[PROF : PROF + 128, :] = paug[:, pl.ds(at, TILE)]
        dep_load(t).wait()
        half = lax.rem(t, 2)
        for n in range(TILE // 256):
            lanes = slice(n * 256, (n + 1) * 256)
            tangent = jnp.dot(jaug[t], xaug[:, lanes], preferred_element_type=F32)
            factor = scale[t, 0:CHAN, :]
            residual = tangent - dep[half, :, lanes].astype(F32)
            forcing[0:CHAN, lanes] = (jnp.concatenate([factor, factor], axis=1) * residual).astype(BF16)
        for n in range(TILE // 256):
            lanes = slice(n * 256, (n + 1) * 256)
            to = pl.multiple_of(at + n * 256, 256)
            value = jnp.dot(jt[t], forcing[:, lanes], preferred_element_type=F32)
            first = value.astype(BF16)
            second = (value - first.astype(F32)).astype(BF16)
            for h in range(LEVD):
                for field in range(NF):
                    rows = slice(field * 128 + h * SLAB, field * 128 + (h + 1) * SLAB)
                    put = slice(field * SLAB, (field + 1) * SLAB)
                    adj[h, 0, put, pl.ds(to, 256)] = first[rows, :]
                    adj[h, 1, put, pl.ds(to, 256)] = second[rows, :]
        return carry

    lax.fori_loop(0, TILES, observe, 0)

    def give_back(step, carry):
        pair = lax.rem(lev // 2 + step // 2, 2)
        half = lax.rem(col // 16 + step, 2)
        acc[...] = jnp.zeros_like(acc)

        def add(t, inner):
            at = pl.multiple_of(t * TILE, TILE)
            left = adj[pl.ds(pair * 2, 2), :, :, pl.ds(at, TILE)].reshape(4 * ROWS, TILE)
            right = jnp.concatenate(
                [
                    hot[pl.ds(pl.multiple_of(owner * 256 + half * 128, 128), 128), pl.ds(at, TILE)]
                    for owner in range(LEVD)
                ],
                axis=0,
            )
            acc[...] += lax.dot_general(
                left, right, (((1,), (1,)), ((), ())), preferred_element_type=F32
            )
            return inner

        lax.fori_loop(0, TILES, add, 0)
        for h in range(2):
            total = acc[h * 192 : h * 192 + ROWS, :] + acc[h * 192 + ROWS : (h + 1) * 192, :]
            tall = jnp.concatenate([total[:, o * 128 : (o + 1) * 128] for o in range(LEVD)], axis=0)
            unit = jnp.max(jnp.abs(tall), axis=0, keepdims=True) * (1.0 / 32767.0)
            per = jnp.where(unit > 1e-37, 1.0 / unit, 0.0)
            units_out[pair * 2 + h, half] = unit
            code = jnp.round(tall * per).T.astype(jnp.int32).astype(jnp.int16)
            rsend[pl.ds((pair * 2 + h) * COLD + half * 16, 16)] = code.reshape(16, CAP, PROF)

        def push(i, inner):
            other = (pair * 2 + i // 16) * COLD + half * 16 + lax.rem(i + col, 16)
            moves = (
                (rsend.at[other], rrecv.at[me], rsend_sem, rrecv_sem),
                (units_out.at[pair * 2 + i // 16, half], units_in.at[me], msend_sem, mrecv_sem),
            )

            @pl.when(other != me)
            def _():
                for src, dst, send, receive in moves:
                    pltpu.make_async_remote_copy(
                        src_ref=src, dst_ref=dst, send_sem=send, recv_sem=receive,
                        device_id=peer_id(other), device_id_type=MESH,
                    ).start()

            @pl.when(other == me)
            def _():
                for n, (src, dst, send, receive) in enumerate(moves):
                    pltpu.make_async_copy(src, dst, own_sem.at[1 + n]).start()

            return inner

        lax.fori_loop(0, 32, push, 0)
        return carry

    lax.fori_loop(0, 4, give_back, 0)
    for owner in range(LEVD):
        build_pick(owner)
    pltpu.make_async_copy(rsend.at[me], rrecv.at[me], own_sem.at[1]).wait()
    pltpu.make_async_copy(units_in.at[me], units_in.at[me], own_sem.at[2]).wait()
    most = pl.ds(0, NDEV - 1)
    for sem in (msend_sem, mrecv_sem):
        pltpu.make_async_copy(units_in.at[most], units_in.at[most], sem).wait()
    pltpu.make_async_copy(rsend.at[most], rsend.at[most], rsend_sem).wait()
    pltpu.make_async_copy(rrecv.at[most], rrecv.at[most], rrecv_sem).wait()
    square[...] = units_in[:, 0, :].T
    units = square[pl.ds(pl.multiple_of(lax.rem(col, 16) * CAP, CAP), CAP), :]
    for m in range(NF):
        rows8[m] = rrecv[:, :, m * 128 : (m + 1) * 128].astype(jnp.int32).astype(F32).reshape(SLOTS, 128)

    for k in range(CAP):
        value = jnp.concatenate([rows8[m, pl.ds(k, NDEV, stride=CAP), :].T for m in range(NF)], axis=0)
        value = value * units[k : k + 1, :]
        first = value.astype(BF16)
        second = (value - first.astype(F32)).astype(BF16)
        lanes = slice(k * 128, (k + 1) * 128)
        for owner in range(LEVD):
            rows = slice(owner * ROWS, (owner + 1) * ROWS)
            yt[owner, 0:ROWS, lanes] = first[rows, :]
            yt[owner, ROWS : 2 * ROWS, lanes] = second[rows, :]
    for owner in range(LEVD):
        both = lax.dot_general(
            yt[owner], hot[:, owner * SLOTS : (owner + 1) * SLOTS], (((1,), (1,)), ((), ())), preferred_element_type=F32
        )
        out_ref[:, owner * COLS : (owner + 1) * COLS] = both[0:ROWS, :] + both[ROWS : 2 * ROWS, :]


def on_device(increment, jacobian, departure, predictor, bias_coef, obs_sigma, channel_use, send_cols, obs_slot):
    out = pl.pallas_call(
        kernel,
        out_shape=jax.ShapeDtypeStruct((ROWS, LEVD * COLS), F32),
        in_specs=[pl.BlockSpec(memory_space=pl.ANY)] * 9,
        out_specs=pl.BlockSpec(memory_space=pltpu.VMEM),
        scratch_shapes=[
            pltpu.VMEM((ROWS, LEVD * COLS), BF16),
            pltpu.VMEM((2, CHAN, TILE), BF16),
            pltpu.VMEM((NPRED, OBS), F32),
            pltpu.VMEM((NPRED, CHAN), F32),
            pltpu.VMEM((CHAN,), F32),
            pltpu.VMEM((TILES, CHAN), jnp.int32),
            pltpu.VMEM((OBS // 128, 128), jnp.int32),
            pltpu.VMEM((LEVD, CAP, NDEV), jnp.int32),
            pltpu.VMEM((SLOTS, OBS), BF16),
            pltpu.VMEM((PROF, SLOTS), F32),
            pltpu.VMEM((NDEV, CAP, PROF), BF16),
            pltpu.VMEM((NDEV, CAP, PROF), BF16),
            pltpu.VMEM((PROF, SLOTS), BF16),
            pltpu.VMEM((PROF + 128, TILE), BF16),
            pltpu.VMEM((TILES, CHAN, PROF + 128), BF16),
            pltpu.VMEM((TILES, PROF, CPAD), BF16),
            pltpu.VMEM((128, OBS), BF16),
            pltpu.VMEM((TILES, CPAD, 128), F32),
            pltpu.VMEM((128, 128), F32),
            pltpu.VMEM((CPAD, TILE), BF16),
            pltpu.VMEM((LEVD, 2, ROWS, OBS), BF16),
            pltpu.VMEM((4 * ROWS, 512), F32),
            pltpu.VMEM((NDEV, CAP, PROF), jnp.int16),
            pltpu.VMEM((NDEV, CAP, PROF), jnp.int16),
            pltpu.VMEM((LEVD, 2, 1, 128), F32),
            pltpu.VMEM((NDEV, 1, 128), F32),
            pltpu.VMEM((NF, SLOTS, 128), F32),
            pltpu.VMEM((LEVD, 2 * ROWS, SLOTS), BF16),
            pltpu.SemaphoreType.DMA((8,)),
            pltpu.SemaphoreType.DMA((2,)),
            pltpu.SemaphoreType.DMA((LEVD,)),
            pltpu.SemaphoreType.DMA((LEVD,)),
            pltpu.SemaphoreType.DMA,
            pltpu.SemaphoreType.DMA,
            pltpu.SemaphoreType.DMA,
            pltpu.SemaphoreType.DMA,
            pltpu.SemaphoreType.DMA,
            pltpu.SemaphoreType.DMA,
            pltpu.SemaphoreType.REGULAR,
            pltpu.SemaphoreType.DMA((3,)),
        ],
        compiler_params=pltpu.CompilerParams(
            collective_id=0, has_side_effects=True, vmem_limit_bytes=63 * 2**20
        ),
    )(
        increment.reshape(ROWS, LEVD * COLS),
        jacobian,
        departure,
        predictor,
        bias_coef.T,
        obs_sigma,
        channel_use,
        send_cols.reshape(NDEV, CAP).T,
        obs_slot.reshape(OBS // 128, 128),
    )
    return out.reshape(NF, SLAB, LEVD * COLS)


def solution(mesh):
    return jax.shard_map(
        on_device,
        mesh=mesh,
        in_specs=(
            P(None, "lev", "col"),
            P(("lev", "col"), None, None),
            P(None, ("lev", "col")),
            P(None, ("lev", "col")),
            P(),
            P(),
            P(("lev", "col"), None),
            P(("lev", "col"), None, None),
            P(("lev", "col")),
        ),
        out_specs=P(None, "lev", "col"),
        check_vma=False,
    )
```

```python
import functools

import jax
import jax.numpy as jnp
from jax import lax
from jax.experimental import pallas as pl
from jax.experimental.pallas import tpu as pltpu
from jax.sharding import PartitionSpec as P

MESH = pl.DeviceIdType.MESH
NF = 3
LEVD = 4
COLD = 32
NDEV = LEVD * COLD
SLAB = 32
ROWS = NF * SLAB
PROF = ROWS * LEVD
CAP = 8
SLOTS = NDEV * CAP
COLS = 1024
CHAN = 616
CPAD = 640
NPRED = 8
TILE = 1024
TILES = 8
OBS = TILE * TILES
PARTS = 2
DEEP = OBS // PARTS
F32 = jnp.float32
BF16 = jnp.bfloat16


def peer_id(index):
    return (index // COLD, lax.rem(index, COLD))


def one_hot(row, block):
    local = jnp.broadcast_to((row - 256.0 * block), (256, 128)).astype(BF16)
    index = lax.broadcasted_iota(jnp.int32, (256, 128), 0).astype(F32).astype(BF16)
    return jnp.where(index == local, jnp.ones((), BF16), jnp.zeros((), BF16))


def split3(value):
    high = value.astype(BF16).astype(F32)
    rest = value - high
    mid = rest.astype(BF16).astype(F32)
    return high, mid, (rest - mid).astype(BF16).astype(F32)


def kernel(
    inc_hbm, jac_hbm, dep_hbm, pred_hbm, coef_hbm, sigma_hbm, use_hbm, cols_hbm, slot_hbm,
    out_ref,
    inc, dep, pred, coef, sigma, use, slot,
    lists, hot, gath, sendb, recvb, xt, xaug, jaug, jt, paug, scale, square, forcing,
    adj, acc, rsend, rrecv, units_out, units_in, rows8, yt,
    in_sem, dep_sem, list_send, list_recv, send_sem, recv_sem, rsend_sem, rrecv_sem, msend_sem, mrecv_sem, all_sem, own_sem,
):
    lev = lax.axis_index("lev")
    col = lax.axis_index("col")
    me = lev * COLD + col
    barrier = pltpu.get_barrier_semaphore()

    loads = [
        pltpu.make_async_copy(src, dst, in_sem.at[i])
        for i, (src, dst) in enumerate(
            (
                (cols_hbm, lists.at[lev]), (inc_hbm, inc), (slot_hbm, slot), (jac_hbm, jaug.at[:, :, pl.ds(0, PROF)]), (pred_hbm, pred),
                (coef_hbm, coef), (sigma_hbm, sigma), (use_hbm, use),
            )
        )
    ]
    for load in loads:
        load.start()

    def dep_load(t):
        at = pl.multiple_of(t * TILE, TILE)
        return pltpu.make_async_copy(
            dep_hbm.at[:, pl.ds(at, TILE)], dep.at[lax.rem(t, 2)], dep_sem.at[lax.rem(t, 2)]
        )

    dep_load(0).start()

    place = col // 2
    core = lax.rem(col, 2)

    def near(i):
        return (lax.rem(lev + i // 2, LEVD), place * 2 + lax.rem(core + i, 2))

    def far(i):
        return (lev, lax.rem(place + i, COLD // 2) * 2 + core)

    for i in range(1, 2 * LEVD):
        pl.semaphore_signal(barrier, inc=1, device_id=near(i), device_id_type=MESH)
    for i in range(1, COLD // 2):
        pl.semaphore_signal(barrier, inc=1, device_id=far(i), device_id_type=MESH)
    def build_pick(owner):
        def build(k, carry):
            row = lists[owner, pl.ds(k, 1), :].astype(F32)
            at = pl.multiple_of(owner * SLOTS + k * 128, 128)
            for b in range(4):
                hot[b * 256 : (b + 1) * 256, pl.ds(at, 128)] = one_hot(row, b)
            return carry

        lax.fori_loop(0, CAP, build, 0)

    def gather(owner):
        build_pick(owner)
        at = pl.multiple_of(owner * COLS, COLS)
        to = pl.multiple_of(owner * ROWS, 32)
        gath[pl.ds(to, ROWS), :] = jnp.dot(
            inc[:, pl.ds(at, COLS)], hot[:, pl.ds(at, SLOTS)], preferred_element_type=F32
        )

    def list_copy(i):
        other = lax.rem(lev + i, LEVD)
        return pltpu.make_async_remote_copy(
            src_ref=lists.at[lev], dst_ref=lists.at[lev], send_sem=list_send.at[i],
            recv_sem=list_recv.at[i], device_id=(other, col), device_id_type=MESH,
        )

    loads[0].wait()
    loads[1].wait()
    gather(lev)
    pl.semaphore_wait(barrier, 2 * LEVD - 1 + COLD // 2 - 1)
    for i in range(1, LEVD):
        list_copy(i).start()
    for i in range(1, 2 * LEVD):
        pl.semaphore_signal(all_sem, inc=1, device_id=near(i), device_id_type=MESH)
    for i in range(1, LEVD):
        list_copy(i).wait_recv()
        gather(lax.rem(lev + (LEVD - i), LEVD))
    for i in range(1, LEVD):
        list_copy(i).wait_send()
    for k in range(CAP):
        for m in range(NF):
            rows8[m, pl.ds(k, NDEV, stride=CAP), :] = gath[m * 128 : (m + 1) * 128, k * 128 : (k + 1) * 128].T
    for m in range(NF):
        sendb[:, :, m * 128 : (m + 1) * 128] = rows8[m].reshape(NDEV, CAP, 128).astype(BF16)

    pl.semaphore_wait(all_sem, 2 * LEVD - 1)
    own = pltpu.make_async_copy(sendb.at[me], recvb.at[me], own_sem.at[0])
    own.start()

    def fetch(i, carry):
        other = lax.rem(me + i, NDEV)
        pltpu.make_async_remote_copy(
            src_ref=sendb.at[other], dst_ref=recvb.at[me], send_sem=send_sem, recv_sem=recv_sem,
            device_id=peer_id(other), device_id_type=MESH,
        ).start()
        return carry

    lax.fori_loop(1, NDEV, fetch, 0)

    for load in loads[2:]:
        load.wait()

    def build_hot(m, carry):
        row = slot[pl.ds(m, 1), :].astype(F32)
        at = pl.multiple_of(m * 128, 128)
        for b in range(4):
            hot[b * 256 : (b + 1) * 256, pl.ds(at, 128)] = one_hot(row, b)
        return carry

    lax.fori_loop(0, OBS // 128, build_hot, 0)

    deviation = sigma[...].reshape(1, CHAN)
    inverse = 1.0 / (deviation * deviation)
    square[...] = jnp.zeros_like(square)
    wide = jnp.concatenate(
        [use[...].astype(F32) * inverse, jnp.zeros((TILES, CPAD - CHAN), F32)], axis=1
    )
    for m in range(CPAD // 128):
        square[0:TILES, :] = wide[:, m * 128 : (m + 1) * 128]
        turned = square[0:128, :].T
        for t in range(TILES):
            scale[t, m * 128 : (m + 1) * 128, :] = jnp.broadcast_to(turned[:, t : t + 1], (128, 128))

    high, mid, low = split3(pred[...])
    paug[...] = jnp.zeros_like(paug)
    paug[0:48, :] = jnp.concatenate([high, mid, low, high, mid, high], axis=0).astype(BF16)
    repeat = (
        lax.broadcasted_iota(jnp.int32, (NPRED, 128), 0)
        == lax.rem(lax.broadcasted_iota(jnp.int32, (NPRED, 128), 1), NPRED)
    ).astype(F32)
    tiled = lax.dot_general(
        coef[...], repeat, (((0,), (0,)), ((), ())), precision=lax.Precision.HIGHEST, preferred_element_type=F32
    )
    ch, cm, cl = split3(tiled)
    lane = lax.broadcasted_iota(jnp.int32, (CHAN, 128), 1)
    ccoef = jnp.where(lane < 24, ch, jnp.where(lane < 40, cm, jnp.where(lane < 48, cl, 0.0)))

    forcing[...] = jnp.zeros_like(forcing)
    for t in range(TILES):
        jaug[t, :, PROF : PROF + 128] = ccoef.astype(BF16)

    def turn(t, carry):
        tall = jnp.concatenate([jaug[t, :, 0:PROF].astype(F32), jnp.zeros((CPAD - CHAN, PROF), F32)], axis=0)
        jt[t] = tall.T.astype(BF16)
        return carry

    lax.fori_loop(0, TILES, turn, 0)

    pltpu.make_async_copy(sendb.at[pl.ds(0, NDEV - 1)], sendb.at[pl.ds(0, NDEV - 1)], send_sem).wait()
    pltpu.make_async_copy(recvb.at[pl.ds(0, NDEV - 1)], recvb.at[pl.ds(0, NDEV - 1)], recv_sem).wait()
    own.wait()
    for h in range(LEVD):
        got = recvb[h * COLD : (h + 1) * COLD].astype(F32).reshape(COLD * CAP, PROF)
        turned = got.T.astype(BF16)
        for owner in range(LEVD):
            for field in range(NF):
                xt[field * 128 + h * SLAB : field * 128 + (h + 1) * SLAB, owner * 256 : (owner + 1) * 256] = turned[
                    owner * ROWS + field * SLAB : owner * ROWS + (field + 1) * SLAB, :
                ]

    def observe(t, carry):
        @pl.when(t + 1 < TILES)
        def _():
            dep_load(t + 1).start()

        at = pl.multiple_of(t * TILE, TILE)
        xaug[0:PROF, :] = jnp.dot(xt[...], hot[:, pl.ds(at, TILE)], preferred_element_type=F32).astype(BF16)
        xaug[PROF : PROF + 128, :] = paug[:, pl.ds(at, TILE)]
        dep_load(t).wait()
        half = lax.rem(t, 2)
        for n in range(TILE // 256):
            lanes = slice(n * 256, (n + 1) * 256)
            tangent = jnp.dot(jaug[t], xaug[:, lanes], preferred_element_type=F32)
            factor = scale[t, 0:CHAN, :]
            residual = tangent - dep[half, :, lanes].astype(F32)
            forcing[0:CHAN, lanes] = (jnp.concatenate([factor, factor], axis=1) * residual).astype(BF16)
        for n in range(TILE // 256):
            lanes = slice(n * 256, (n + 1) * 256)
            to = pl.multiple_of(at + n * 256, 256)
            value = jnp.dot(jt[t], forcing[:, lanes], preferred_element_type=F32)
            first = value.astype(BF16)
            second = (value - first.astype(F32)).astype(BF16)
            for h in range(LEVD):
                for field in range(NF):
                    rows = slice(field * 128 + h * SLAB, field * 128 + (h + 1) * SLAB)
                    put = slice(field * SLAB, (field + 1) * SLAB)
                    adj[h, 0, put, pl.ds(to, 256)] = first[rows, :]
                    adj[h, 1, put, pl.ds(to, 256)] = second[rows, :]
        return carry

    lax.fori_loop(0, TILES, observe, 0)

    plane = col // 8
    offsets = (2, 1, 3, 0)

    def push(step, i):
        row = lax.rem(lev + i // 8, LEVD)
        other = row * COLD + lax.rem(plane + offsets[step], 4) * 8 + lax.rem(col + i, 8)
        for src, dst, send, receive in (
            (rsend.at[other], rrecv.at[me], rsend_sem, rrecv_sem),
            (units_out.at[step, row // 2], units_in.at[me], msend_sem, mrecv_sem),
        ):
            pltpu.make_async_remote_copy(
                src_ref=src, dst_ref=dst, send_sem=send, recv_sem=receive,
                device_id=peer_id(other), device_id_type=MESH,
            ).start()

    for step in range(4):
        target = lax.rem(plane + offsets[step], 4)

        def add(t, inner):
            if step:
                for n in range(32 // PARTS):
                    push(step - 1, t * (32 // PARTS) + n)
            at = pl.multiple_of(t * DEEP, DEEP)
            left = adj[:, :, :, pl.ds(at, DEEP)].reshape(8 * ROWS, DEEP)
            right = jnp.concatenate(
                [
                    hot[pl.ds(pl.multiple_of(owner * 256 + target * 64, 64), 64), pl.ds(at, DEEP)]
                    for owner in range(LEVD)
                ],
                axis=0,
            )
            more = lax.dot_general(left, right, (((1,), (1,)), ((), ())), preferred_element_type=F32)

            acc[...] += more
            return inner

        acc[...] = jnp.zeros_like(acc)
        lax.fori_loop(0, PARTS, add, 0)
        for pair in range(2):
            parts = []
            for h in (2 * pair, 2 * pair + 1):
                total = acc[h * 192 : h * 192 + ROWS, :] + acc[h * 192 + ROWS : (h + 1) * 192, :]
                parts.append(
                    jnp.concatenate([total[:, o * 64 : (o + 1) * 64] for o in range(LEVD)], axis=0)
                )
            tall = jnp.concatenate(parts, axis=1)
            unit = jnp.max(jnp.abs(tall), axis=0, keepdims=True) * (1.0 / 32767.0)
            per = jnp.where(unit > 1e-37, 1.0 / unit, 0.0)
            units_out[step, pair] = unit
            code = jnp.round(tall * per).T.astype(jnp.int32).astype(jnp.int16)
            for h in range(2):
                rsend[pl.ds((2 * pair + h) * COLD + target * 8, 8)] = code[h * 64 : (h + 1) * 64, :].reshape(
                    8, CAP, PROF
                )

    kept = (
        pltpu.make_async_copy(rsend.at[me], rrecv.at[me], own_sem.at[1]),
        pltpu.make_async_copy(units_out.at[3, lev // 2], units_in.at[me], own_sem.at[2]),
    )

    def last(i, carry):
        push(3, i)
        return carry

    lax.fori_loop(1, 32, last, 0)
    for copy in kept:
        copy.start()
    for owner in range(LEVD):
        build_pick(owner)
    for copy in kept:
        copy.wait()
    most = pl.ds(0, NDEV - 1)
    for sem in (msend_sem, mrecv_sem):
        pltpu.make_async_copy(units_in.at[most], units_in.at[most], sem).wait()
    pltpu.make_async_copy(rsend.at[most], rsend.at[most], rsend_sem).wait()
    pltpu.make_async_copy(rrecv.at[most], rrecv.at[most], rrecv_sem).wait()
    square[...] = units_in[:, 0, :].T
    units = square[pl.ds(pl.multiple_of(lax.rem(lev, 2) * 64 + lax.rem(col, 8) * CAP, CAP), CAP), :]
    for m in range(NF):
        rows8[m] = rrecv[:, :, m * 128 : (m + 1) * 128].astype(jnp.int32).astype(F32).reshape(SLOTS, 128)

    for k in range(CAP):
        value = jnp.concatenate([rows8[m, pl.ds(k, NDEV, stride=CAP), :].T for m in range(NF)], axis=0)
        value = value * units[k : k + 1, :]
        first = value.astype(BF16)
        second = (value - first.astype(F32)).astype(BF16)
        lanes = slice(k * 128, (k + 1) * 128)
        for owner in range(LEVD):
            rows = slice(owner * ROWS, (owner + 1) * ROWS)
            yt[owner, 0:ROWS, lanes] = first[rows, :]
            yt[owner, ROWS : 2 * ROWS, lanes] = second[rows, :]
    for owner in range(LEVD):
        both = lax.dot_general(
            yt[owner], hot[:, owner * SLOTS : (owner + 1) * SLOTS], (((1,), (1,)), ((), ())), preferred_element_type=F32
        )
        out_ref[:, owner * COLS : (owner + 1) * COLS] = both[0:ROWS, :] + both[ROWS : 2 * ROWS, :]


def on_device(increment, jacobian, departure, predictor, bias_coef, obs_sigma, channel_use, send_cols, obs_slot):
    out = pl.pallas_call(
        kernel,
        out_shape=jax.ShapeDtypeStruct((ROWS, LEVD * COLS), F32),
        in_specs=[pl.BlockSpec(memory_space=pl.ANY)] * 9,
        out_specs=pl.BlockSpec(memory_space=pltpu.VMEM),
        scratch_shapes=[
            pltpu.VMEM((ROWS, LEVD * COLS), BF16),
            pltpu.VMEM((2, CHAN, TILE), BF16),
            pltpu.VMEM((NPRED, OBS), F32),
            pltpu.VMEM((NPRED, CHAN), F32),
            pltpu.VMEM((CHAN,), F32),
            pltpu.VMEM((TILES, CHAN), jnp.int32),
            pltpu.VMEM((OBS // 128, 128), jnp.int32),
            pltpu.VMEM((LEVD, CAP, NDEV), jnp.int32),
            pltpu.VMEM((SLOTS, OBS), BF16),
            pltpu.VMEM((PROF, SLOTS), F32),
            pltpu.VMEM((NDEV, CAP, PROF), BF16),
            pltpu.VMEM((NDEV, CAP, PROF), BF16),
            pltpu.VMEM((PROF, SLOTS), BF16),
            pltpu.VMEM((PROF + 128, TILE), BF16),
            pltpu.VMEM((TILES, CHAN, PROF + 128), BF16),
            pltpu.VMEM((TILES, PROF, CPAD), BF16),
            pltpu.VMEM((128, OBS), BF16),
            pltpu.VMEM((TILES, CPAD, 128), F32),
            pltpu.VMEM((128, 128), F32),
            pltpu.VMEM((CPAD, TILE), BF16),
            pltpu.VMEM((LEVD, 2, ROWS, OBS), BF16),
            pltpu.VMEM((8 * ROWS, 256), F32),
            pltpu.VMEM((NDEV, CAP, PROF), jnp.int16),
            pltpu.VMEM((NDEV, CAP, PROF), jnp.int16),
            pltpu.VMEM((4, 2, 1, 128), F32),
            pltpu.VMEM((NDEV, 1, 128), F32),
            pltpu.VMEM((NF, SLOTS, 128), F32),
            pltpu.VMEM((LEVD, 2 * ROWS, SLOTS), BF16),
            pltpu.SemaphoreType.DMA((8,)),
            pltpu.SemaphoreType.DMA((2,)),
            pltpu.SemaphoreType.DMA((LEVD,)),
            pltpu.SemaphoreType.DMA((LEVD,)),
            pltpu.SemaphoreType.DMA,
            pltpu.SemaphoreType.DMA,
            pltpu.SemaphoreType.DMA,
            pltpu.SemaphoreType.DMA,
            pltpu.SemaphoreType.DMA,
            pltpu.SemaphoreType.DMA,
            pltpu.SemaphoreType.REGULAR,
            pltpu.SemaphoreType.DMA((3,)),
        ],
        compiler_params=pltpu.CompilerParams(
            collective_id=0, has_side_effects=True, vmem_limit_bytes=63 * 2**20
        ),
    )(
        increment.reshape(ROWS, LEVD * COLS),
        jacobian,
        departure,
        predictor,
        bias_coef.T,
        obs_sigma,
        channel_use,
        send_cols.reshape(NDEV, CAP).T,
        obs_slot.reshape(OBS // 128, 128),
    )
    return out.reshape(NF, SLAB, LEVD * COLS)


def solution(mesh):
    return jax.shard_map(
        on_device,
        mesh=mesh,
        in_specs=(
            P(None, "lev", "col"),
            P(("lev", "col"), None, None),
            P(None, ("lev", "col")),
            P(None, ("lev", "col")),
            P(),
            P(),
            P(("lev", "col"), None),
            P(("lev", "col"), None, None),
            P(("lev", "col")),
        ),
        out_specs=P(None, "lev", "col"),
        check_vma=False,
    )
```

```python
import functools

import jax
import jax.numpy as jnp
from jax import lax
from jax.experimental import pallas as pl
from jax.experimental.pallas import tpu as pltpu
from jax.sharding import PartitionSpec as P

MESH = pl.DeviceIdType.MESH
NF = 3
LEVD = 4
COLD = 32
NDEV = LEVD * COLD
SLAB = 32
ROWS = NF * SLAB
PROF = ROWS * LEVD
CAP = 8
SLOTS = NDEV * CAP
COLS = 1024
CHAN = 616
CPAD = 640
NPRED = 8
TILE = 1024
TILES = 8
OBS = TILE * TILES
PARTS = 2
DEEP = OBS // PARTS
F32 = jnp.float32
BF16 = jnp.bfloat16


def peer_id(index):
    return (index // COLD, lax.rem(index, COLD))


def one_hot(row, block):
    local = jnp.broadcast_to((row - 256.0 * block), (256, 128)).astype(BF16)
    index = lax.broadcasted_iota(jnp.int32, (256, 128), 0).astype(F32).astype(BF16)
    return jnp.where(index == local, jnp.ones((), BF16), jnp.zeros((), BF16))


def split3(value):
    high = value.astype(BF16).astype(F32)
    rest = value - high
    mid = rest.astype(BF16).astype(F32)
    return high, mid, (rest - mid).astype(BF16).astype(F32)


def kernel(
    inc_hbm, jac_hbm, dep_hbm, pred_hbm, coef_hbm, sigma_hbm, use_hbm, cols_hbm, slot_hbm,
    out_ref,
    inc, dep, pred, coef, sigma, use, slot,
    lists, hot, gath, sendb, recvb, xt, xaug, jaug, jt, paug, scale, square, forcing,
    adj, acc, rsend, rrecv, units_out, units_in, rows8, yt,
    in_sem, dep_sem, list_send, list_recv, send_sem, recv_sem, rsend_sem, rrecv_sem, msend_sem, mrecv_sem, all_sem, own_sem,
):
    lev = lax.axis_index("lev")
    col = lax.axis_index("col")
    me = lev * COLD + col
    barrier = pltpu.get_barrier_semaphore()

    loads = [
        pltpu.make_async_copy(src, dst, in_sem.at[i])
        for i, (src, dst) in enumerate(
            (
                (cols_hbm, lists.at[lev]), (inc_hbm, inc), (slot_hbm, slot), (jac_hbm, jaug.at[:, :, pl.ds(0, PROF)]), (pred_hbm, pred),
                (coef_hbm, coef), (sigma_hbm, sigma), (use_hbm, use),
            )
        )
    ]
    for load in loads:
        load.start()

    def dep_load(t):
        at = pl.multiple_of(t * TILE, TILE)
        return pltpu.make_async_copy(
            dep_hbm.at[:, pl.ds(at, TILE)], dep.at[lax.rem(t, 2)], dep_sem.at[lax.rem(t, 2)]
        )

    dep_load(0).start()

    place = col // 2
    core = lax.rem(col, 2)

    def near(i):
        return (lax.rem(lev + i // 2, LEVD), place * 2 + lax.rem(core + i, 2))

    def far(i):
        return (lev, lax.rem(place + i, COLD // 2) * 2 + core)

    for i in range(1, 2 * LEVD):
        pl.semaphore_signal(barrier, inc=1, device_id=near(i), device_id_type=MESH)
    for i in range(1, COLD // 2):
        pl.semaphore_signal(barrier, inc=1, device_id=far(i), device_id_type=MESH)
    def build_pick(owner):
        def build(k, carry):
            row = lists[owner, pl.ds(k, 1), :].astype(F32)
            at = pl.multiple_of(owner * SLOTS + k * 128, 128)
            for b in range(4):
                hot[b * 256 : (b + 1) * 256, pl.ds(at, 128)] = one_hot(row, b)
            return carry

        lax.fori_loop(0, CAP, build, 0)

    def gather(owner):
        build_pick(owner)
        at = pl.multiple_of(owner * COLS, COLS)
        to = pl.multiple_of(owner * ROWS, 32)
        gath[pl.ds(to, ROWS), :] = jnp.dot(
            inc[:, pl.ds(at, COLS)], hot[:, pl.ds(at, SLOTS)], preferred_element_type=F32
        )

    def list_copy(i):
        other = lax.rem(lev + i, LEVD)
        return pltpu.make_async_remote_copy(
            src_ref=lists.at[lev], dst_ref=lists.at[lev], send_sem=list_send.at[i],
            recv_sem=list_recv.at[i], device_id=(other, col), device_id_type=MESH,
        )

    loads[0].wait()
    loads[1].wait()
    gather(lev)
    pl.semaphore_wait(barrier, 2 * LEVD - 1 + COLD // 2 - 1)
    for i in range(1, LEVD):
        list_copy(i).start()
    for i in range(1, 2 * LEVD):
        pl.semaphore_signal(all_sem, inc=1, device_id=near(i), device_id_type=MESH)
    for i in range(1, LEVD):
        list_copy(i).wait_recv()
        gather(lax.rem(lev + (LEVD - i), LEVD))
    for i in range(1, LEVD):
        list_copy(i).wait_send()
    for k in range(CAP):
        for m in range(NF):
            rows8[m, pl.ds(k, NDEV, stride=CAP), :] = gath[m * 128 : (m + 1) * 128, k * 128 : (k + 1) * 128].T
    for m in range(NF):
        sendb[:, :, m * 128 : (m + 1) * 128] = rows8[m].reshape(NDEV, CAP, 128).astype(BF16)

    pl.semaphore_wait(all_sem, 2 * LEVD - 1)
    own = pltpu.make_async_copy(sendb.at[me], recvb.at[me], own_sem.at[0])
    own.start()

    def fetch(i, carry):
        other = lax.rem(me + i, NDEV)
        pltpu.make_async_remote_copy(
            src_ref=sendb.at[other], dst_ref=recvb.at[me], send_sem=send_sem, recv_sem=recv_sem,
            device_id=peer_id(other), device_id_type=MESH,
        ).start()
        return carry

    lax.fori_loop(1, NDEV, fetch, 0)

    for load in loads[2:]:
        load.wait()

    def build_hot(m, carry):
        row = slot[pl.ds(m, 1), :].astype(F32)
        at = pl.multiple_of(m * 128, 128)
        for b in range(4):
            hot[b * 256 : (b + 1) * 256, pl.ds(at, 128)] = one_hot(row, b)
        return carry

    lax.fori_loop(0, OBS // 128, build_hot, 0)

    deviation = sigma[...].reshape(1, CHAN)
    inverse = 1.0 / (deviation * deviation)
    square[...] = jnp.zeros_like(square)
    wide = jnp.concatenate(
        [use[...].astype(F32) * inverse, jnp.zeros((TILES, CPAD - CHAN), F32)], axis=1
    )
    for m in range(CPAD // 128):
        square[0:TILES, :] = wide[:, m * 128 : (m + 1) * 128]
        turned = square[0:128, :].T
        for t in range(TILES):
            scale[t, m * 128 : (m + 1) * 128, :] = jnp.broadcast_to(turned[:, t : t + 1], (128, 128))

    high, mid, low = split3(pred[...])
    paug[...] = jnp.zeros_like(paug)
    paug[0:48, :] = jnp.concatenate([high, mid, low, high, mid, high], axis=0).astype(BF16)
    repeat = (
        lax.broadcasted_iota(jnp.int32, (NPRED, 128), 0)
        == lax.rem(lax.broadcasted_iota(jnp.int32, (NPRED, 128), 1), NPRED)
    ).astype(F32)
    tiled = lax.dot_general(
        coef[...], repeat, (((0,), (0,)), ((), ())), precision=lax.Precision.HIGHEST, preferred_element_type=F32
    )
    ch, cm, cl = split3(tiled)
    lane = lax.broadcasted_iota(jnp.int32, (CHAN, 128), 1)
    ccoef = jnp.where(lane < 24, ch, jnp.where(lane < 40, cm, jnp.where(lane < 48, cl, 0.0)))

    forcing[...] = jnp.zeros_like(forcing)
    for t in range(TILES):
        jaug[t, :, PROF : PROF + 128] = ccoef.astype(BF16)

    def turn(t, carry):
        tall = jnp.concatenate([jaug[t, :, 0:PROF].astype(F32), jnp.zeros((CPAD - CHAN, PROF), F32)], axis=0)
        jt[t] = tall.T.astype(BF16)
        return carry

    lax.fori_loop(0, TILES, turn, 0)

    pltpu.make_async_copy(sendb.at[pl.ds(0, NDEV - 1)], sendb.at[pl.ds(0, NDEV - 1)], send_sem).wait()
    pltpu.make_async_copy(recvb.at[pl.ds(0, NDEV - 1)], recvb.at[pl.ds(0, NDEV - 1)], recv_sem).wait()
    own.wait()
    for h in range(LEVD):
        got = recvb[h * COLD : (h + 1) * COLD].astype(F32).reshape(COLD * CAP, PROF)
        turned = got.T.astype(BF16)
        for owner in range(LEVD):
            for field in range(NF):
                xt[field * 128 + h * SLAB : field * 128 + (h + 1) * SLAB, owner * 256 : (owner + 1) * 256] = turned[
                    owner * ROWS + field * SLAB : owner * ROWS + (field + 1) * SLAB, :
                ]

    def observe(t, carry):
        @pl.when(t + 1 < TILES)
        def _():
            dep_load(t + 1).start()

        at = pl.multiple_of(t * TILE, TILE)
        xaug[0:PROF, :] = jnp.dot(xt[...], hot[:, pl.ds(at, TILE)], preferred_element_type=F32).astype(BF16)
        xaug[PROF : PROF + 128, :] = paug[:, pl.ds(at, TILE)]
        dep_load(t).wait()
        half = lax.rem(t, 2)
        for n in range(TILE // 512):
            lanes = slice(n * 512, (n + 1) * 512)
            tangent = jnp.dot(jaug[t], xaug[:, lanes], preferred_element_type=F32)
            factor = scale[t, 0:CHAN, :]
            residual = tangent - dep[half, :, lanes].astype(F32)
            forcing[0:CHAN, lanes] = (jnp.concatenate([factor] * 4, axis=1) * residual).astype(BF16)
        for n in range(TILE // 512):
            lanes = slice(n * 512, (n + 1) * 512)
            to = pl.multiple_of(at + n * 512, 512)
            value = jnp.dot(jt[t], forcing[:, lanes], preferred_element_type=F32)
            first = value.astype(BF16)
            second = (value - first.astype(F32)).astype(BF16)
            for h in range(LEVD):
                for field in range(NF):
                    rows = slice(field * 128 + h * SLAB, field * 128 + (h + 1) * SLAB)
                    put = slice(field * SLAB, (field + 1) * SLAB)
                    adj[h, 0, put, pl.ds(to, 512)] = first[rows, :]
                    adj[h, 1, put, pl.ds(to, 512)] = second[rows, :]
        return carry

    lax.fori_loop(0, TILES, observe, 0)

    plane = col // 8
    offsets = (2, 1, 3, 0)

    def push(step, i):
        row = lax.rem(lev + i // 8, LEVD)
        other = row * COLD + lax.rem(plane + offsets[step], 4) * 8 + lax.rem(col + i, 8)
        for src, dst, send, receive in (
            (rsend.at[other], rrecv.at[me], rsend_sem, rrecv_sem),
            (units_out.at[step, row // 2], units_in.at[me], msend_sem, mrecv_sem),
        ):
            pltpu.make_async_remote_copy(
                src_ref=src, dst_ref=dst, send_sem=send, recv_sem=receive,
                device_id=peer_id(other), device_id_type=MESH,
            ).start()

    for step in range(4):
        target = lax.rem(plane + offsets[step], 4)

        def add(t, inner):
            if step:
                for n in range(32 // PARTS):
                    push(step - 1, t * (32 // PARTS) + n)
            at = pl.multiple_of(t * DEEP, DEEP)
            left = adj[:, :, :, pl.ds(at, DEEP)].reshape(8 * ROWS, DEEP)
            right = jnp.concatenate(
                [
                    hot[pl.ds(pl.multiple_of(owner * 256 + target * 64, 64), 64), pl.ds(at, DEEP)]
                    for owner in range(LEVD)
                ],
                axis=0,
            )
            more = lax.dot_general(left, right, (((1,), (1,)), ((), ())), preferred_element_type=F32)

            acc[...] += more
            return inner

        acc[...] = jnp.zeros_like(acc)
        lax.fori_loop(0, PARTS, add, 0)
        for pair in range(2):
            parts = []
            for h in (2 * pair, 2 * pair + 1):
                total = acc[h * 192 : h * 192 + ROWS, :] + acc[h * 192 + ROWS : (h + 1) * 192, :]
                parts.append(
                    jnp.concatenate([total[:, o * 64 : (o + 1) * 64] for o in range(LEVD)], axis=0)
                )
            tall = jnp.concatenate(parts, axis=1)
            unit = jnp.max(jnp.abs(tall), axis=0, keepdims=True) * (1.0 / 32767.0)
            per = jnp.where(unit > 1e-37, 1.0 / unit, 0.0)
            units_out[step, pair] = unit
            code = jnp.round(tall * per).T.astype(jnp.int32).astype(jnp.int16)
            for h in range(2):
                rsend[pl.ds((2 * pair + h) * COLD + target * 8, 8)] = code[h * 64 : (h + 1) * 64, :].reshape(
                    8, CAP, PROF
                )

    kept = (
        pltpu.make_async_copy(rsend.at[me], rrecv.at[me], own_sem.at[1]),
        pltpu.make_async_copy(units_out.at[3, lev // 2], units_in.at[me], own_sem.at[2]),
    )

    def last(i, carry):
        push(3, i)
        return carry

    lax.fori_loop(1, 32, last, 0)
    for copy in kept:
        copy.start()
    for owner in range(LEVD):
        build_pick(owner)
    for copy in kept:
        copy.wait()
    most = pl.ds(0, NDEV - 1)
    for sem in (msend_sem, mrecv_sem):
        pltpu.make_async_copy(units_in.at[most], units_in.at[most], sem).wait()
    pltpu.make_async_copy(rsend.at[most], rsend.at[most], rsend_sem).wait()
    pltpu.make_async_copy(rrecv.at[most], rrecv.at[most], rrecv_sem).wait()
    square[...] = units_in[:, 0, :].T
    units = square[pl.ds(pl.multiple_of(lax.rem(lev, 2) * 64 + lax.rem(col, 8) * CAP, CAP), CAP), :]
    for m in range(NF):
        rows8[m] = rrecv[:, :, m * 128 : (m + 1) * 128].astype(jnp.int32).astype(F32).reshape(SLOTS, 128)

    for k in range(CAP):
        value = jnp.concatenate([rows8[m, pl.ds(k, NDEV, stride=CAP), :].T for m in range(NF)], axis=0)
        value = value * units[k : k + 1, :]
        first = value.astype(BF16)
        second = (value - first.astype(F32)).astype(BF16)
        lanes = slice(k * 128, (k + 1) * 128)
        for owner in range(LEVD):
            rows = slice(owner * ROWS, (owner + 1) * ROWS)
            yt[owner, 0:ROWS, lanes] = first[rows, :]
            yt[owner, ROWS : 2 * ROWS, lanes] = second[rows, :]
    for owner in range(LEVD):
        both = lax.dot_general(
            yt[owner], hot[:, owner * SLOTS : (owner + 1) * SLOTS], (((1,), (1,)), ((), ())), preferred_element_type=F32
        )
        out_ref[:, owner * COLS : (owner + 1) * COLS] = both[0:ROWS, :] + both[ROWS : 2 * ROWS, :]


def on_device(increment, jacobian, departure, predictor, bias_coef, obs_sigma, channel_use, send_cols, obs_slot):
    out = pl.pallas_call(
        kernel,
        out_shape=jax.ShapeDtypeStruct((ROWS, LEVD * COLS), F32),
        in_specs=[pl.BlockSpec(memory_space=pl.ANY)] * 9,
        out_specs=pl.BlockSpec(memory_space=pltpu.VMEM),
        scratch_shapes=[
            pltpu.VMEM((ROWS, LEVD * COLS), BF16),
            pltpu.VMEM((2, CHAN, TILE), BF16),
            pltpu.VMEM((NPRED, OBS), F32),
            pltpu.VMEM((NPRED, CHAN), F32),
            pltpu.VMEM((CHAN,), F32),
            pltpu.VMEM((TILES, CHAN), jnp.int32),
            pltpu.VMEM((OBS // 128, 128), jnp.int32),
            pltpu.VMEM((LEVD, CAP, NDEV), jnp.int32),
            pltpu.VMEM((SLOTS, OBS), BF16),
            pltpu.VMEM((PROF, SLOTS), F32),
            pltpu.VMEM((NDEV, CAP, PROF), BF16),
            pltpu.VMEM((NDEV, CAP, PROF), BF16),
            pltpu.VMEM((PROF, SLOTS), BF16),
            pltpu.VMEM((PROF + 128, TILE), BF16),
            pltpu.VMEM((TILES, CHAN, PROF + 128), BF16),
            pltpu.VMEM((TILES, PROF, CPAD), BF16),
            pltpu.VMEM((128, OBS), BF16),
            pltpu.VMEM((TILES, CPAD, 128), F32),
            pltpu.VMEM((128, 128), F32),
            pltpu.VMEM((CPAD, TILE), BF16),
            pltpu.VMEM((LEVD, 2, ROWS, OBS), BF16),
            pltpu.VMEM((8 * ROWS, 256), F32),
            pltpu.VMEM((NDEV, CAP, PROF), jnp.int16),
            pltpu.VMEM((NDEV, CAP, PROF), jnp.int16),
            pltpu.VMEM((4, 2, 1, 128), F32),
            pltpu.VMEM((NDEV, 1, 128), F32),
            pltpu.VMEM((NF, SLOTS, 128), F32),
            pltpu.VMEM((LEVD, 2 * ROWS, SLOTS), BF16),
            pltpu.SemaphoreType.DMA((8,)),
            pltpu.SemaphoreType.DMA((2,)),
            pltpu.SemaphoreType.DMA((LEVD,)),
            pltpu.SemaphoreType.DMA((LEVD,)),
            pltpu.SemaphoreType.DMA,
            pltpu.SemaphoreType.DMA,
            pltpu.SemaphoreType.DMA,
            pltpu.SemaphoreType.DMA,
            pltpu.SemaphoreType.DMA,
            pltpu.SemaphoreType.DMA,
            pltpu.SemaphoreType.REGULAR,
            pltpu.SemaphoreType.DMA((3,)),
        ],
        compiler_params=pltpu.CompilerParams(
            collective_id=0, has_side_effects=True, vmem_limit_bytes=63 * 2**20
        ),
    )(
        increment.reshape(ROWS, LEVD * COLS),
        jacobian,
        departure,
        predictor,
        bias_coef.T,
        obs_sigma,
        channel_use,
        send_cols.reshape(NDEV, CAP).T,
        obs_slot.reshape(OBS // 128, 128),
    )
    return out.reshape(NF, SLAB, LEVD * COLS)


def solution(mesh):
    return jax.shard_map(
        on_device,
        mesh=mesh,
        in_specs=(
            P(None, "lev", "col"),
            P(("lev", "col"), None, None),
            P(None, ("lev", "col")),
            P(None, ("lev", "col")),
            P(),
            P(),
            P(("lev", "col"), None),
            P(("lev", "col"), None, None),
            P(("lev", "col")),
        ),
        out_specs=P(None, "lev", "col"),
        check_vma=False,
    )
```
